32 devices in a mesh: lon: 8 (over z, x), lat: 4 (over y, core).
Axes of the slice: x: 2, y: 2, z: 4, core: 2. Of those that a mesh axis runs over, the one named last changes fastest.
Arguments:
- thick: float32 [4, 768, 5760], P(None, 'lat', 'lon'), may hold values from 0.5 to 1.5
- uwind: float32 [4, 768, 5760], P(None, 'lat', 'lon'), may hold values from -3 to 3
- vwind: float32 [4, 768, 5760], P(None, 'lat', 'lon'), may hold values from -3 to 3
- theta: float32 [4, 768, 5760], P(None, 'lat', 'lon'), may hold values from -4 to 4
- moist: float32 [4, 768, 5760], P(None, 'lat', 'lon'), may hold values from -4 to 4
- lon_courant: float32 [768], P('lat'), may hold values from 0.05 to 0.5
- lat_courant: float32 [], replicated, may hold values from 0.2 to 0.5
- coriolis: float32 [768], P('lat'), may hold values from -0.5 to 0.5
- cap_mask: int32 [768], P('lat'), may hold values from 0 to 1, as said below
- cutoffs: int32 [768], P('lat'), may hold values from 1 to 255, as said below
Outputs:
- thick_new: float32 [4, 768, 5760], P(None, 'lat', 'lon')
- uwind_new: float32 [4, 768, 5760], P(None, 'lat', 'lon')
- vwind_new: float32 [4, 768, 5760], P(None, 'lat', 'lon')
- theta_mass: float32 [4, 768, 5760], P(None, 'lat', 'lon')
- moist_mass: float32 [4, 768, 5760], P(None, 'lat', 'lon')
The draws below stay inside these ranges and needn't reach their ends.
Inputs may be any that keep to these rules, and one draw needn't show every extreme that they name: `cap_mask`: 0 on all rows outside the first 32 and the last 32 rows; the first and the last row hold 1. `cutoffs`: row 0 holds 255.
All inputs are finite; a program needn't handle non-finite values.
Results may differ from the reference program's by a relative error of at most 0.000098.
Values sent between devices are 32-bit elements; how exact they have to be, the bound alone decides.
A program may use at most 192 MiB of HBM per device.

```python
import math
import jax
import jax.numpy as jnp
from jax import lax

NLON = 5760
LEV = 4
CAP = 32
KEEP = 256
NLAT = 768


def draw_cap_mask(key, part):
    picks = jax.random.randint(jax.random.fold_in(key, 11), (NLAT,), 0, 2)
    rows = jnp.arange(NLAT, dtype=jnp.int32)
    inside = (rows < CAP) | (rows >= NLAT - CAP)
    chosen = inside & (picks != 0)
    chosen = chosen | (rows == 0) | (rows == NLAT - 1)
    return chosen.astype(jnp.int32)


def draw_cutoffs(key, part):
    values = jax.random.randint(jax.random.fold_in(key, 23), (NLAT,), 1, KEEP)
    return values.at[0].set(KEEP - 1).astype(jnp.int32)


def block_scale(own_key, extent, cuts, smallest, top_value):
    def one(dim, blocks):
        steps = jax.random.uniform(jax.random.fold_in(jax.random.fold_in(own_key, 6), dim), (blocks,), jnp.float32, smallest / len(cuts), top_value / len(cuts))
        return jnp.repeat(jnp.exp(steps), extent[dim] // blocks).reshape((-1,) + (1,) * (len(extent) - dim - 1))

    loudness = one(*cuts[0])
    for cut in cuts[1:]:
        loudness = loudness * one(*cut)
    return loudness


def centred(rng, dims, deviation, bound, cuts=(), kind=jnp.bfloat16):
    array = jax.random.normal(rng, dims, jnp.float32) * deviation
    if len(cuts) > 0:
        array = block_scale(rng, dims, cuts, -0.22, 0.18) * array
    return jnp.clip(array, min=-bound, max=bound).astype(kind)


def setup_inputs(seed: int = 0) -> dict:
    splits = jax.random.split(jax.random.key(seed), 11)
    return {
        "thick": jnp.clip(0.5 + 1.0 * jax.random.uniform(splits[0], (LEV, NLAT, NLON), jnp.float32) ** block_scale(splits[0], (LEV, NLAT, NLON), ((1, 4), (2, 8)), -0.2, 0.2), 0.5, 1.5),
        "uwind": centred(splits[1], (LEV, NLAT, NLON), 1.0, 3.0, ((1, 4), (2, 8)), jnp.float32),
        "vwind": centred(splits[2], (LEV, NLAT, NLON), 1.0, 3.0, ((1, 4), (2, 8)), jnp.float32),
        "theta": centred(splits[3], (LEV, NLAT, NLON), 1.0, 4.0, ((1, 4), (2, 8)), jnp.float32),
        "moist": centred(splits[4], (LEV, NLAT, NLON), 1.0, 4.0, ((1, 4), (2, 8)), jnp.float32),
        "lon_courant": jnp.clip(jnp.exp(math.log(0.5) - 2.3025851 * jax.random.uniform(splits[5], (NLAT,), jnp.float32) ** block_scale(splits[5], (NLAT,), ((0, 4),), -0.2, 0.2)), 0.05, 0.5),
        "lat_courant": jnp.clip(jax.random.uniform(splits[6], (), jnp.float32, 0.2, 0.5), 0.2, 0.5),
        "coriolis": jnp.clip(jax.random.uniform(splits[7], (NLAT,), jnp.float32, -0.5, 0.5) * block_scale(splits[7], (NLAT,), ((0, 4),), -0.4, 0.0), -0.5, 0.5),
        "cap_mask": draw_cap_mask(jax.random.fold_in(splits[10], 71), 0),
        "cutoffs": draw_cutoffs(jax.random.fold_in(splits[10], 71), 0),
    }


def window(source, lower, length, along):
    return lax.slice_in_dim(source, lower, lower + length, axis=along)


def flux_divergence(masses, winds, courant, along):
    length = masses.shape[along] - 4
    face_speed = courant * 0.5 * (window(winds, 1, length + 1, along) + window(winds, 2, length + 1, along))
    left = window(masses, 1, length + 1, along)
    right = window(masses, 2, length + 1, along)
    face_value = (7.0 * (left + right) - (window(masses, 0, length + 1, along) + window(masses, 3, length + 1, along))) / 12.0
    face_flux = face_speed * face_value - 0.5 * jnp.abs(face_speed) * (right - left)
    return window(face_flux, 1, length, along) - window(face_flux, 0, length, along)


def centered(source, along):
    length = source.shape[along] - 4
    return 0.5 * (window(source, 3, length, along) - window(source, 1, length, along))


def middle(source, along):
    length = source.shape[along] - 4
    return window(source, 2, length, along)


def tendencies(lonpad, latpad, lon_courant, lat_courant, coriolis):
    zonal_axis = lonpad.ndim - 2
    merid_axis = zonal_axis - 1
    zonal = lon_courant[:, None]
    rotation = coriolis[:, None]
    thick_lon = lonpad[0]
    thick_lat = latpad[0]
    lon_masses = (thick_lon, thick_lon * lonpad[3], thick_lon * lonpad[4])
    lat_masses = (thick_lat, thick_lat * latpad[3], thick_lat * latpad[4])
    tend_masses = [-(flux_divergence(lon_mass, lonpad[1], zonal, zonal_axis) + flux_divergence(lat_mass, latpad[2], lat_courant, merid_axis)) for lon_mass, lat_mass in zip(lon_masses, lat_masses)]
    zonal_wind = middle(lonpad[1], zonal_axis)
    merid_wind = middle(lonpad[2], zonal_axis)
    tend_u = -zonal * zonal_wind * centered(lonpad[1], zonal_axis) - lat_courant * merid_wind * centered(latpad[1], merid_axis) - zonal * centered(thick_lon, zonal_axis) + rotation * merid_wind
    tend_v = -zonal * zonal_wind * centered(lonpad[2], zonal_axis) - lat_courant * merid_wind * centered(latpad[2], merid_axis) - lat_courant * centered(thick_lat, merid_axis) - rotation * zonal_wind
    return tend_masses[0], tend_u, tend_v, tend_masses[1], tend_masses[2]


def reference(thick, uwind, vwind, theta, moist, lon_courant, lat_courant, coriolis, cap_mask, cutoffs):
    fields = jnp.stack([thick, uwind, vwind, theta, moist], 1)

    def per_level(level_fields):
        lonpad = jnp.concatenate([level_fields[..., -2:], level_fields, level_fields[..., :2]], -1)
        latpad = jnp.pad(level_fields, ((0, 0), (2, 2), (0, 0)))
        return jnp.stack(tendencies(lonpad, latpad, lon_courant, lat_courant, coriolis))

    tend = lax.map(per_level, fields)
    increment = tend[:, :3]
    spectra = jnp.fft.rfft(increment, axis=-1)[..., :KEEP]
    modes = jnp.arange(KEEP, dtype=jnp.int32)
    kept_modes = modes[None, :] <= cutoffs[:, None]
    filtered = jnp.fft.irfft(jnp.where(kept_modes, spectra, 0.0), n=NLON, axis=-1)
    increment = jnp.where((cap_mask == 1)[:, None], filtered, increment)
    thick_new = thick + increment[:, 0]
    uwind_new = uwind + increment[:, 1]
    vwind_new = vwind + increment[:, 2]
    theta_mass = thick * theta + tend[:, 3]
    moist_mass = thick * moist + tend[:, 4]
    return (thick_new, uwind_new, vwind_new, theta_mass, moist_mass)
```

```python
import functools
import math

import jax
import jax.numpy as jnp
import ml_dtypes
import numpy as np
from jax import lax
from jax.experimental import pallas as pl
from jax.experimental.pallas import tpu as pltpu
from jax.sharding import PartitionSpec as P

CAP = 32
KEEP = 256
RANK = 128
VMEM_LIMIT = 60 * 1024 * 1024


def split_table(table):
    table = np.asarray(table, np.float32)
    high = table.astype(ml_dtypes.bfloat16)
    low = (table - high.astype(np.float32)).astype(ml_dtypes.bfloat16)
    return high, low


@functools.lru_cache(maxsize=None)
def tables(cells, count, padded):
    full = cells * count
    t = np.arange(cells)
    band = (KEEP - 0.5) / full
    diag = ((cells - 1 - 2 * t) / 2.0) ** 2 * math.cos(2 * math.pi * band)
    off = t[1:] * (cells - t[1:]) / 2.0
    _, vectors = np.linalg.eigh(np.diag(diag) + np.diag(off, 1) + np.diag(off, -1))
    basis = vectors[:, ::-1][:, :RANK]
    basis = basis * np.where(basis[cells // 2 - 3] < 0, -1.0, 1.0)
    modes = np.arange(KEEP)
    blocks = []
    for s in range(count):
        phase = 2 * np.pi * (((s * cells + t)[:, None] * modes[None, :]) % full) / full
        blocks.append(basis.T @ np.concatenate([np.cos(phase), np.sin(phase)], 1))
    wide = np.zeros((padded, RANK))
    wide[:cells] = basis
    return split_table(wide) + split_table(wide.T) + split_table(np.concatenate(blocks, 0))


def halves(x):
    high = x.astype(jnp.bfloat16)
    return high, (x - high.astype(jnp.float32)).astype(jnp.bfloat16)


def dot3(x, high, low, rhs_dim=0):
    dims = (((1,), (rhs_dim,)), ((), ()))
    xh, xl = halves(x)
    dot = functools.partial(
        lax.dot_general, dimension_numbers=dims, preferred_element_type=jnp.float32
    )
    return dot(xh, high) + (dot(xl, high) + dot(xh, low))


def row_ids(width):
    return lax.broadcasted_iota(jnp.int32, (8, width), 0)


def row_up(cur, nxt, k, rows):
    return pltpu.roll(jnp.where(rows < k, nxt, cur), 8 - k, 0)


def row_down(cur, prv, k, rows):
    return pltpu.roll(jnp.where(rows >= 8 - k, prv, cur), k, 0)


def lane(x, k):
    return pltpu.roll(x, (-k) % x.shape[1], 1)


def face_terms(speed):
    part = speed * (1.0 / 12.0)
    seven = 7.0 * part
    half = 0.5 * jnp.abs(speed)
    return seven + half, seven - half, part


def lat_flux(load, r, b, masses, rows):
    v, vn = load(2, r), load(2, r + 8)
    p, q, s = face_terms((0.5 * b) * (v + row_up(v, vn, 1, rows)))
    out = []
    for m in masses:
        prv, cur, nxt = load(m, r - 8), load(m, r), load(m, r + 8)
        out.append(
            p * cur
            + q * row_up(cur, nxt, 1, rows)
            - s * (row_down(cur, prv, 1, rows) + row_up(cur, nxt, 2, rows))
        )
    return out


def chunk(load, r, a, f, b, masses, carry, rows):
    h, u, v = load(0, r), load(1, r), load(2, r)
    ue, uw = lane(u, 1), lane(u, -1)
    p, q, s = face_terms((0.5 * a) * (u + ue))
    fluxes = lat_flux(load, r, b, masses, rows)
    tends = []
    dh = None
    for m, up, before in zip(masses, fluxes, carry):
        cur = load(m, r)
        east, west = lane(cur, 1), lane(cur, -1)
        if m == 0:
            dh = east - west
        flux = p * cur + q * east - s * (west + lane(cur, 2))
        tends.append(lane(flux, -1) - flux + (row_down(up, before, 1, rows) - up))
    au, bv = (0.5 * a) * u, (0.5 * b) * v

    def across(m):
        prv, cur, nxt = load(m, r - 8), load(m, r), load(m, r + 8)
        return row_up(cur, nxt, 1, rows) - row_down(cur, prv, 1, rows)

    tend_u = f * v - au * (ue - uw) - bv * across(1) - (0.5 * a) * dh
    tend_v = (
        -(f * u) - au * (lane(v, 1) - lane(v, -1)) - bv * across(2) - (0.5 * b) * across(0)
    )
    return tends, tend_u, tend_v, fluxes


def widen(x, width, east, west, east_shift, west_shift):
    cells = x.shape[1]
    last = width - 128
    tail = jnp.concatenate(
        [x[:, last:], jnp.zeros((x.shape[0], width - cells), jnp.float32)], 1
    )
    ids = lax.broadcasted_iota(jnp.int32, (x.shape[0], 128), 1)
    e = cells - last
    tail = jnp.where((ids >= e) & (ids < e + 2), pltpu.roll(east, east_shift, 1), tail)
    tail = jnp.where(ids >= 126, pltpu.roll(west, west_shift, 1), tail)
    return x[:, :last], tail


def exchange_kernel(geo, *refs):
    lev, n_rows, cells, width, count, bands = geo
    left, right = refs[0:5], refs[5:10]
    fields = refs[10:15]
    par, lat_c, cuts, uh, ul, gh, gl = refs[15:22]
    out_east, out_west, out_north, out_south, out_coef = refs[22:27]
    (
        send_w, send_e, got_e, got_w, edge_n, edge_s, send_n, send_s, got_n, got_s,
        cap_raw, cap, cap_t, comp, mid_in, mid_out, coef,
        in_sem, lon_send, lon_recv, lat_send, lat_recv, a_send, a_recv, b_send, b_recv,
    ) = refs[27:]
    me = lax.axis_index("lon")
    band = lax.axis_index("lat")
    has_n = band > 0
    has_s = band < bands - 1
    is_cap = jnp.logical_or(band == 0, band == bands - 1)
    last = width - 128
    e = cells - last
    owned = 3 * lev * CAP // count

    barrier = pltpu.get_barrier_semaphore()
    for j in range(1, count):
        pl.semaphore_signal(barrier, inc=1, device_id={"lon": lax.rem(me + j, count)})

    @pl.when(has_n)
    def _():
        pl.semaphore_signal(barrier, inc=1, device_id={"lat": band - 1})

    @pl.when(has_s)
    def _():
        pl.semaphore_signal(barrier, inc=1, device_id={"lat": band + 1})

    cap_row = jnp.where(band == 0, 0, n_rows - CAP - 8)
    loads = []
    for k in range(5):
        loads.append(
            pltpu.make_async_copy(fields[k].at[:, pl.ds(0, 8), :], edge_n.at[k], in_sem.at[k])
        )
        loads.append(
            pltpu.make_async_copy(
                fields[k].at[:, pl.ds(n_rows - 8, 8), :], edge_s.at[k], in_sem.at[5 + k]
            )
        )
    cap_loads = [
        pltpu.make_async_copy(
            fields[k].at[:, pl.ds(pl.multiple_of(cap_row, 8), CAP + 8), :],
            cap_raw.at[k],
            in_sem.at[10 + k],
        )
        for k in range(3)
    ]
    for copy in loads + cap_loads:
        copy.start()

    ids = lax.broadcasted_iota(jnp.int32, (n_rows, 128), 1)
    west_edge = jnp.zeros((n_rows, 128), jnp.float32)
    east_edge = jnp.zeros((n_rows, 128), jnp.float32)
    for k in range(5):
        for level in range(lev):
            at = 2 * (5 * level + k)
            here = (ids >= at) & (ids < at + 2)
            west_edge = jnp.where(here, pltpu.roll(left[k][level], at, 1), west_edge)
            east_edge = jnp.where(
                here, pltpu.roll(right[k][level], (at - (e - 2)) % 128, 1), east_edge
            )
    send_w[...] = west_edge
    send_e[...] = east_edge

    greeted = count - 1 + jnp.where(has_n, 1, 0) + jnp.where(has_s, 1, 0)
    pl.semaphore_wait(barrier, greeted)

    to_west = pltpu.make_async_remote_copy(
        src_ref=send_w, dst_ref=got_e, send_sem=lon_send.at[0], recv_sem=lon_recv.at[0],
        device_id={"lon": lax.rem(me + count - 1, count)},
    )
    to_east = pltpu.make_async_remote_copy(
        src_ref=send_e, dst_ref=got_w, send_sem=lon_send.at[1], recv_sem=lon_recv.at[1],
        device_id={"lon": lax.rem(me + 1, count)},
    )
    to_west.start()
    to_east.start()

    for copy in loads:
        copy.wait()
    for k in range(5):
        for level in range(lev):
            send_n[level, 2 * k : 2 * k + 2, :] = edge_n[k, level, 0:2, :]
            send_s[level, 2 * k : 2 * k + 2, :] = edge_s[k, level, 6:8, :]
    to_north = pltpu.make_async_remote_copy(
        src_ref=send_n, dst_ref=got_s, send_sem=lat_send.at[0], recv_sem=lat_recv.at[0],
        device_id={"lat": lax.rem(band + bands - 1, bands)},
    )
    to_south = pltpu.make_async_remote_copy(
        src_ref=send_s, dst_ref=got_n, send_sem=lat_send.at[1], recv_sem=lat_recv.at[1],
        device_id={"lat": lax.rem(band + 1, bands)},
    )

    @pl.when(has_n)
    def _():
        to_north.start()

    @pl.when(has_s)
    def _():
        to_south.start()

    for copy in cap_loads:
        copy.wait()
    to_west.wait()
    to_east.wait()
    out_east[...] = got_e[...]
    out_west[...] = got_w[...]

    @pl.when(is_cap)
    def _():
        rows = row_ids(width)
        b = lat_c[0]
        halo_row = pl.multiple_of(cap_row, 8)
        for k in range(3):
            for level in range(lev):
                at = 2 * (5 * level + k)
                body, tail = widen(
                    cap_raw[k, level], width,
                    got_e[pl.ds(halo_row, CAP + 8), :], got_w[pl.ds(halo_row, CAP + 8), :],
                    (e - at) % 128, (126 - at) % 128,
                )
                cap[k, level, 0:8, :] = jnp.zeros((8, width), jnp.float32)
                cap[k, level, 8 : CAP + 16, :last] = body
                cap[k, level, 8 : CAP + 16, last:] = tail
                cap[k, level, CAP + 16 : CAP + 24, :] = jnp.zeros((8, width), jnp.float32)
        first = jnp.where(band == 0, 8, 16)

        def level_body(level, _):
            def load(m, r):
                return cap[m, level, pl.ds(pl.multiple_of(r, 8), 8), :]

            def body(c, carry):
                r = first + 8 * c
                pr = pl.multiple_of(jnp.where(band == 0, 0, n_rows - CAP) + 8 * c, 8)
                a = par[pl.ds(pr, 8), 0:1]
                f = par[pl.ds(pr, 8), 1:2]
                tends, tu, tv, fluxes = chunk(load, r, a, f, b, (0,), carry, rows)
                dst = pl.multiple_of(8 * c, 8)
                cap_t[0, level, pl.ds(dst, 8), :] = tends[0]
                cap_t[1, level, pl.ds(dst, 8), :] = tu
                cap_t[2, level, pl.ds(dst, 8), :] = tv
                return fluxes

            v, vn = load(2, first - 8), load(2, first)
            p, q, s = face_terms((0.5 * b) * (v + row_up(v, vn, 1, rows)))
            cur, nxt = load(0, first - 8), load(0, first)
            before = (
                p * cur
                + q * row_up(cur, nxt, 1, rows)
                - s * (row_down(cur, cur, 1, rows) + row_up(cur, nxt, 2, rows))
            )
            lax.fori_loop(0, CAP // 8, body, [before])
            return 0

        lax.fori_loop(0, lev, level_body, 0)
        flat = cap_t[...].reshape(3 * lev * CAP, width)
        comp[...] = dot3(flat, uh[...], ul[...]).reshape(count, owned, RANK)

        def send(src, dst, sends, recvs, j):
            peer = lax.rem(me + j, count)
            return pltpu.make_async_remote_copy(
                src_ref=src.at[peer], dst_ref=dst.at[me],
                send_sem=sends.at[j], recv_sem=recvs.at[j], device_id={"lon": peer},
            )

        first_sends = [send(comp, mid_in, a_send, a_recv, j) for j in range(1, count)]
        for copy in first_sends:
            copy.start()
        mid_in[me] = comp[me]
        for copy in first_sends:
            copy.wait()
        spectra = None
        for s in range(count):
            part = pl.ds(s * RANK, RANK)
            term = dot3(mid_in[s], gh[part, :], gl[part, :])
            spectra = term if spectra is None else spectra + term
        modes = lax.broadcasted_iota(jnp.int32, (owned, 2 * KEEP), 1)
        modes = jnp.where(modes >= KEEP, modes - KEEP, modes)
        full = cells * count
        weight = jnp.where(modes == 0, 1.0 / full, 2.0 / full).astype(jnp.float32)
        limit = cuts[pl.ds(pl.multiple_of(me * owned, 8), owned), 0:1]
        spectra = jnp.where(modes.astype(jnp.float32) <= limit, spectra * weight, 0.0)
        for s in range(count):
            part = pl.ds(s * RANK, RANK)
            mid_out[s] = dot3(spectra, gh[part, :], gl[part, :], 1)
        second_sends = [send(mid_out, coef, b_send, b_recv, j) for j in range(1, count)]
        for copy in second_sends:
            copy.start()
        coef[me] = mid_out[me]
        for copy in second_sends:
            copy.wait()
        out_coef[...] = coef[...].reshape(3 * lev * CAP, RANK)

    @pl.when(jnp.logical_not(is_cap))
    def _():
        out_coef[...] = jnp.zeros((3 * lev * CAP, RANK), jnp.float32)

    @pl.when(has_n)
    def _():
        to_north.wait_send()
        to_south_in = to_south
        to_south_in.wait_recv()
        out_north[...] = got_n[...]

    @pl.when(has_s)
    def _():
        to_south.wait_send()
        to_north.wait_recv()
        out_south[...] = got_s[...]

    @pl.when(jnp.logical_not(has_n))
    def _():
        out_north[...] = jnp.zeros(out_north.shape, jnp.float32)

    @pl.when(jnp.logical_not(has_s))
    def _():
        out_south[...] = jnp.zeros(out_south.shape, jnp.float32)


def step_kernel(geo, *refs):
    lev, n_rows, cells, width, count, bands = geo
    fields = refs[0:5]
    par, lat_c, east, west, north, south, coef, wh, wl = refs[5:14]
    outs = refs[14:19]
    pad = refs[19]
    level = pl.program_id(0)
    band = lax.axis_index("lat")
    last = width - 128
    e = cells - last
    rows = row_ids(width)
    b = lat_c[0]
    for k in range(5):
        pad[k, 0:8, :] = jnp.zeros((8, width), jnp.float32)
        pad[k, n_rows + 8 : n_rows + 16, :] = jnp.zeros((8, width), jnp.float32)
        pad[k, 6:8, :cells] = north[0, 2 * k : 2 * k + 2, :]
        pad[k, n_rows + 8 : n_rows + 10, :cells] = south[0, 2 * k : 2 * k + 2, :]
    for k in (3, 4):
        for r in (0, n_rows + 8):
            pad[k, r : r + 8, :] = pad[k, r : r + 8, :] * pad[0, r : r + 8, :]

    def fill(c, _):
        r = pl.multiple_of(8 * c, 8)
        to = pl.multiple_of(8 * c + 8, 8)
        ea, we = east[pl.ds(r, 8), :], west[pl.ds(r, 8), :]
        thick = None
        for k in range(5):
            at = 2 * (5 * level + k)
            body, tail = widen(
                fields[k][0, pl.ds(r, 8), :], width, ea, we,
                e + 128 - at, 126 - at,
            )
            if k == 0:
                thick = body, tail
            if k >= 3:
                body, tail = body * thick[0], tail * thick[1]
            pad[k, pl.ds(to, 8), :last] = body
            pad[k, pl.ds(to, 8), last:] = tail
        return 0

    lax.fori_loop(0, n_rows // 8, fill, 0)

    def load(m, r):
        return pad[m, pl.ds(pl.multiple_of(r, 8), 8), :]

    masses = (0, 3, 4)
    v, vn = load(2, 0), load(2, 8)
    p, q, s = face_terms((0.5 * b) * (v + row_up(v, vn, 1, rows)))
    before = []
    for m in masses:
        cur, nxt = load(m, 0), load(m, 8)
        before.append(
            p * cur
            + q * row_up(cur, nxt, 1, rows)
            - s * (row_down(cur, cur, 1, rows) + row_up(cur, nxt, 2, rows))
        )

    def body(c, carry):
        r = 8 * c + 8
        src = pl.multiple_of(8 * c, 8)
        a = par[pl.ds(src, 8), 0:1]
        f = par[pl.ds(src, 8), 1:2]
        tends, tu, tv, fluxes = chunk(load, r, a, f, b, masses, carry, rows)
        for k, t in zip(range(5), (tends[0], tu, tv, tends[1], tends[2])):
            outs[k][0, pl.ds(src, 8), :] = (load(k, r) + t)[:, :cells]
        return fluxes

    lax.fori_loop(0, n_rows // 8, body, before)

    @pl.when(jnp.logical_or(band == 0, band == bands - 1))
    def _():
        start = pl.multiple_of(jnp.where(band == 0, 0, n_rows - CAP), 8)
        flat = coef[...].reshape(3 * CAP, RANK)
        smooth = dot3(flat, wh[...], wl[...])
        chosen = par[pl.ds(start, CAP), 2:3] == 1.0
        for k in range(3):
            new = fields[k][0, pl.ds(start, CAP), :] + smooth[CAP * k : CAP * k + CAP, :cells]
            old = outs[k][0, pl.ds(start, CAP), :]
            outs[k][0, pl.ds(start, CAP), :] = jnp.where(chosen, new, old)


def local(thick, uwind, vwind, theta, moist, lon_courant, lat_courant, coriolis, cap_mask, cutoffs):
    lev, n_rows, cells = thick.shape
    count = lax.axis_size("lon")
    bands = lax.axis_size("lat")
    width = (cells + 4 + 127) // 128 * 128
    geo = (lev, n_rows, cells, width, count, bands)
    uh, ul, wh, wl, gh, gl = (jnp.asarray(t) for t in tables(cells, count, width))
    fields = (thick, uwind, vwind, theta, moist)
    par = jnp.stack(
        [lon_courant, coriolis, (cap_mask == 1).astype(jnp.float32)], 1
    )
    cap_cuts = jnp.where(
        lax.axis_index("lat") == 0, cutoffs[:CAP], cutoffs[n_rows - CAP :]
    ).astype(jnp.float32)
    cuts = jnp.tile(cap_cuts, 3 * lev)[:, None]
    lat_c = lat_courant.reshape(1)

    whole = lambda shape: pl.BlockSpec(shape, lambda i: (0,) * len(shape))
    smem = pl.BlockSpec(memory_space=pltpu.SMEM)
    edge = lambda col: pl.BlockSpec((lev, n_rows, 128), lambda i: (0, 0, col))
    owned = 3 * lev * CAP // count
    f32 = jnp.float32
    rows_all = 3 * lev * CAP
    dma = pltpu.SemaphoreType.DMA
    east, west, north, south, coef = pl.pallas_call(
        functools.partial(exchange_kernel, geo),
        grid=(1,),
        out_shape=(
            jax.ShapeDtypeStruct((n_rows, 128), f32),
            jax.ShapeDtypeStruct((n_rows, 128), f32),
            jax.ShapeDtypeStruct((lev, 10, cells), f32),
            jax.ShapeDtypeStruct((lev, 10, cells), f32),
            jax.ShapeDtypeStruct((rows_all, RANK), f32),
        ),
        in_specs=[edge(0)] * 5
        + [edge(cells // 128)] * 5
        + [pl.BlockSpec(memory_space=pl.ANY)] * 5
        + [whole(par.shape), smem, whole(cuts.shape)]
        + [whole(t.shape) for t in (uh, ul, gh, gl)],
        out_specs=(
            whole((n_rows, 128)),
            whole((n_rows, 128)),
            whole((lev, 10, cells)),
            whole((lev, 10, cells)),
            whole((rows_all, RANK)),
        ),
        scratch_shapes=[pltpu.VMEM((n_rows, 128), f32)] * 4
        + [pltpu.VMEM((5, lev, 8, cells), f32)] * 2
        + [pltpu.VMEM((lev, 10, cells), f32)] * 4
        + [
            pltpu.VMEM((3, lev, CAP + 8, cells), f32),
            pltpu.VMEM((3, lev, CAP + 24, width), f32),
            pltpu.VMEM((3, lev, CAP, width), f32),
        ]
        + [pltpu.VMEM((count, owned, RANK), f32)] * 4
        + [dma((13,))]
        + [dma((2,))] * 4
        + [dma((count,))] * 4,
        compiler_params=pltpu.CompilerParams(
            collective_id=0, has_side_effects=True, vmem_limit_bytes=VMEM_LIMIT
        ),
        name="exchange",
    )(*fields, *fields, *fields, par, lat_c, cuts, uh, ul, gh, gl)

    by_level = lambda shape: pl.BlockSpec(
        (1,) + shape, lambda i: (i,) + (0,) * len(shape)
    )
    coef = coef.reshape(3, lev, CAP, RANK)
    return pl.pallas_call(
        functools.partial(step_kernel, geo),
        grid=(lev,),
        out_shape=tuple(jax.ShapeDtypeStruct((lev, n_rows, cells), f32) for _ in range(5)),
        in_specs=[by_level((n_rows, cells))] * 5
        + [whole(par.shape), smem, whole((n_rows, 128)), whole((n_rows, 128))]
        + [by_level((10, cells))] * 2
        + [pl.BlockSpec((3, 1, CAP, RANK), lambda i: (0, i, 0, 0))]
        + [whole(wh.shape)] * 2,
        out_specs=[by_level((n_rows, cells))] * 5,
        scratch_shapes=[pltpu.VMEM((5, n_rows + 16, width), f32)],
        compiler_params=pltpu.CompilerParams(vmem_limit_bytes=VMEM_LIMIT),
        name="substep",
    )(*fields, par, lat_c, east, west, north, south, coef, wh, wl)


def solution(mesh):
    field = P(None, "lat", "lon")
    row = P("lat")
    return jax.shard_map(
        local,
        mesh=mesh,
        in_specs=(field,) * 5 + (row, P(), row, row, row),
        out_specs=(field,) * 5,
        check_vma=False,
    )
```

```python
import functools
import math

import jax
import jax.numpy as jnp
import ml_dtypes
import numpy as np
from jax import lax
from jax.experimental import pallas as pl
from jax.experimental.pallas import tpu as pltpu
from jax.sharding import PartitionSpec as P

CAP = 32
KEEP = 256
RANK = 128
VMEM_LIMIT = 60 * 1024 * 1024


def split_table(table):
    table = np.asarray(table, np.float32)
    high = table.astype(ml_dtypes.bfloat16)
    low = (table - high.astype(np.float32)).astype(ml_dtypes.bfloat16)
    return high, low


@functools.lru_cache(maxsize=None)
def tables(cells, count, padded):
    full = cells * count
    t = np.arange(cells)
    band = (KEEP - 0.5) / full
    diag = ((cells - 1 - 2 * t) / 2.0) ** 2 * math.cos(2 * math.pi * band)
    off = t[1:] * (cells - t[1:]) / 2.0
    _, vectors = np.linalg.eigh(np.diag(diag) + np.diag(off, 1) + np.diag(off, -1))
    basis = vectors[:, ::-1][:, :RANK]
    basis = basis * np.where(basis[cells // 2 - 3] < 0, -1.0, 1.0)
    modes = np.arange(KEEP)
    blocks = []
    for s in range(count):
        phase = 2 * np.pi * (((s * cells + t)[:, None] * modes[None, :]) % full) / full
        blocks.append(basis.T @ np.concatenate([np.cos(phase), np.sin(phase)], 1))
    wide = np.zeros((padded, RANK))
    wide[:cells] = basis
    modal = np.concatenate(blocks, 0)
    return (
        split_table(wide) + split_table(wide.T) + split_table(modal) + split_table(modal.T)
    )


def halves(x):
    high = x.astype(jnp.bfloat16)
    return high, (x - high.astype(jnp.float32)).astype(jnp.bfloat16)


def dot3(x, high, low):
    dot = functools.partial(jnp.dot, preferred_element_type=jnp.float32)
    xh, xl = halves(x)
    rows = x.shape[0]
    both = dot(jnp.concatenate([xh, xl], 0), high)
    return both[:rows] + (both[rows:] + dot(xh, low))


def eight_rows(vector, first, rows):
    out = jnp.full(rows.shape, vector[first])
    for k in range(1, 8):
        out = jnp.where(rows == k, vector[first + k], out)
    return out


def row_up(cur, nxt, k, rows):
    return pltpu.roll(jnp.where(rows < k, nxt, cur), 8 - k, 0)


def row_down(cur, prv, k, rows):
    return pltpu.roll(jnp.where(rows >= 8 - k, prv, cur), k, 0)


def lane_up(cur, nxt, k, lanes):
    return pltpu.roll(jnp.where(lanes < k, nxt, cur), 128 - k, 1)


def lane_down(cur, prv, k, lanes):
    return pltpu.roll(jnp.where(lanes >= 128 - k, prv, cur), k, 1)


def tile_ids():
    return (
        lax.broadcasted_iota(jnp.int32, (8, 128), 0),
        lax.broadcasted_iota(jnp.int32, (8, 128), 1),
    )


def face_terms(speed):
    part = speed * (1.0 / 12.0)
    seven = 7.0 * part
    half = 0.5 * jnp.abs(speed)
    return seven + half, seven - half, part


def first_carry(load, r, b, masses, tiles, carry):
    rows, _ = tile_ids()
    for c in range(tiles):
        v, vn = load(2, r, c), load(2, r + 8, c)
        p, q, s = face_terms((0.5 * b) * (v + row_up(v, vn, 1, rows)))
        for k, m in enumerate(masses):
            cur, nxt = load(m, r, c), load(m, r + 8, c)
            carry[k, :, 128 * c : 128 * c + 128] = (
                p * cur
                + q * row_up(cur, nxt, 1, rows)
                - s * (row_down(cur, cur, 1, rows) + row_up(cur, nxt, 2, rows))
            )


def rolled(load, tiles):
    lanes = tile_ids()[1]

    def near(m, r, c, k):
        cur = load(m, r, c)
        if k > 0:
            return lane_up(cur, load(m, r, (c + 1) % tiles), k, lanes)
        return lane_down(cur, load(m, r, (c + tiles - 1) % tiles), -k, lanes)

    return near


def shift_tables():
    eye = np.eye(128)
    out = []
    for pair in ((1, 2), (1, -1)):
        moves = np.concatenate([np.roll(eye, -k, 0).T for k in pair], 1)
        out.append(np.concatenate([moves, moves], 0).astype(ml_dtypes.bfloat16))
    return np.stack(out)


def chunk(load, near, r, a, f, b, masses, tiles, carry, emit):
    rows, lanes = tile_ids()
    half_a = 0.5 * a

    def lon_part(c):
        ue = near(1, r, c, 1)
        p, q, s = face_terms(half_a * (load(1, r, c) + ue))
        fluxes, dh = [], None
        for m in masses:
            e, w = near(m, r, c, 1), near(m, r, c, -1)
            if m == 0:
                dh = e - w
            fluxes.append(p * load(m, r, c) + q * e - s * (w + near(m, r, c, 2)))
        return fluxes, dh, ue

    wrapped = lon_part(tiles - 1)
    before = wrapped[0]
    for c in range(tiles):
        fluxes, dh, ue = wrapped if c == tiles - 1 else lon_part(c)
        cols = slice(128 * c, 128 * c + 128)
        u, v = load(1, r, c), load(2, r, c)
        vn = row_up(v, load(2, r + 8, c), 1, rows)
        p, q, s = face_terms((0.5 * b) * (v + vn))
        tends = []
        dn = None
        for k, m in enumerate(masses):
            prv, cur, nxt = load(m, r - 8, c), load(m, r, c), load(m, r + 8, c)
            n, so = row_up(cur, nxt, 1, rows), row_down(cur, prv, 1, rows)
            if m == 0:
                dn = n - so
            up = p * cur + q * n - s * (so + row_up(cur, nxt, 2, rows))
            tends.append(
                lane_down(fluxes[k], before[k], 1, lanes)
                - fluxes[k]
                + (row_down(up, carry[k, :, cols], 1, rows) - up)
            )
            carry[k, :, cols] = up
        before = fluxes
        au, bv = half_a * u, (0.5 * b) * v
        du = row_up(u, load(1, r + 8, c), 1, rows) - row_down(u, load(1, r - 8, c), 1, rows)
        dv = vn - row_down(v, load(2, r - 8, c), 1, rows)
        tu = f * v - au * (ue - near(1, r, c, -1)) - bv * du - half_a * dh
        tv = -(f * u) - au * (near(2, r, c, 1) - near(2, r, c, -1)) - bv * dv - (0.5 * b) * dn
        emit(c, [tends[0], tu, tv] + tends[1:])


def widen(x, width, east, west, east_shift, west_shift):
    cells = x.shape[1]
    last = width - 128
    tail = jnp.concatenate(
        [x[:, last:], jnp.zeros((x.shape[0], width - cells), jnp.float32)], 1
    )
    ids = lax.broadcasted_iota(jnp.int32, (x.shape[0], 128), 1)
    e = cells - last
    tail = jnp.where((ids >= e) & (ids < e + 2), pltpu.roll(east, east_shift, 1), tail)
    tail = jnp.where(ids >= 126, pltpu.roll(west, west_shift, 1), tail)
    return x[:, :last], tail


def exchange_kernel(geo, *refs):
    lev, n_rows, cells, width, count, bands = geo
    left, right = refs[0:5], refs[5:10]
    fields = refs[10:15]
    courant, rotate, cuts, lat_c, uh, ul = refs[15:21]
    in_hbm = refs[21:25]
    out_east, out_west, out_north, out_south, out_coef = refs[25:30]
    (
        send_w, send_e, got_e, got_w, edge_n, edge_s, send_n, send_s, got_n, got_s,
        cap_raw, cap, cap_t, carry, gh, gl, th, tl, comp, mid_in, mid_out, coef,
        in_sem, lon_send, lon_recv, lat_send, lat_recv, a_send, a_recv, b_send, b_recv,
    ) = refs[30:]
    me = lax.axis_index("lon")
    band = lax.axis_index("lat")
    has_n = band > 0
    has_s = band < bands - 1
    is_cap = jnp.logical_or(band == 0, band == bands - 1)
    last = width - 128
    e = cells - last
    owned = 3 * lev * CAP // count

    barrier = pltpu.get_barrier_semaphore()
    for j in range(1, count):
        pl.semaphore_signal(barrier, inc=1, device_id={"lon": lax.rem(me + j, count)})

    @pl.when(has_n)
    def _():
        pl.semaphore_signal(barrier, inc=1, device_id={"lat": band - 1})

    @pl.when(has_s)
    def _():
        pl.semaphore_signal(barrier, inc=1, device_id={"lat": band + 1})

    cap_row = jnp.where(band == 0, 0, n_rows - CAP - 8)
    loads = []
    for k in range(5):
        loads.append(
            pltpu.make_async_copy(fields[k].at[:, pl.ds(0, 8), :], edge_n.at[k], in_sem.at[k])
        )
        loads.append(
            pltpu.make_async_copy(
                fields[k].at[:, pl.ds(n_rows - 8, 8), :], edge_s.at[k], in_sem.at[5 + k]
            )
        )
    cap_loads = [
        pltpu.make_async_copy(
            fields[k].at[:, pl.ds(pl.multiple_of(cap_row, 8), CAP + 8), :],
            cap_raw.at[k],
            in_sem.at[10 + k],
        )
        for k in range(3)
    ]
    table_loads = [
        pltpu.make_async_copy(src, dst, in_sem.at[13 + k])
        for k, (src, dst) in enumerate(zip(in_hbm, (gh, gl, th, tl)))
    ]
    for copy in loads + cap_loads + table_loads:
        copy.start()

    ids = lax.broadcasted_iota(jnp.int32, (n_rows, 128), 1)
    west_edge = jnp.zeros((n_rows, 128), jnp.float32)
    east_edge = jnp.zeros((n_rows, 128), jnp.float32)
    for k in range(5):
        for level in range(lev):
            at = 2 * (5 * level + k)
            here = (ids >= at) & (ids < at + 2)
            west_edge = jnp.where(here, pltpu.roll(left[k][level], at, 1), west_edge)
            east_edge = jnp.where(
                here, pltpu.roll(right[k][level], (at - (e - 2)) % 128, 1), east_edge
            )
    send_w[...] = west_edge
    send_e[...] = east_edge

    greeted = count - 1 + jnp.where(has_n, 1, 0) + jnp.where(has_s, 1, 0)
    pl.semaphore_wait(barrier, greeted)

    to_west = pltpu.make_async_remote_copy(
        src_ref=send_w, dst_ref=got_e, send_sem=lon_send.at[0], recv_sem=lon_recv.at[0],
        device_id={"lon": lax.rem(me + count - 1, count)},
    )
    to_east = pltpu.make_async_remote_copy(
        src_ref=send_e, dst_ref=got_w, send_sem=lon_send.at[1], recv_sem=lon_recv.at[1],
        device_id={"lon": lax.rem(me + 1, count)},
    )
    to_west.start()
    to_east.start()

    for copy in loads:
        copy.wait()
    for k in range(5):
        for level in range(lev):
            send_n[level, 2 * k : 2 * k + 2, :] = edge_n[k, level, 0:2, :]
            send_s[level, 2 * k : 2 * k + 2, :] = edge_s[k, level, 6:8, :]
    to_north = pltpu.make_async_remote_copy(
        src_ref=send_n, dst_ref=got_s, send_sem=lat_send.at[0], recv_sem=lat_recv.at[0],
        device_id={"lat": lax.rem(band + bands - 1, bands)},
    )
    to_south = pltpu.make_async_remote_copy(
        src_ref=send_s, dst_ref=got_n, send_sem=lat_send.at[1], recv_sem=lat_recv.at[1],
        device_id={"lat": lax.rem(band + 1, bands)},
    )

    @pl.when(has_n)
    def _():
        to_north.start()

    @pl.when(has_s)
    def _():
        to_south.start()

    for copy in cap_loads:
        copy.wait()
    to_west.wait()
    to_east.wait()
    out_east[...] = got_e[...]
    out_west[...] = got_w[...]

    for copy in table_loads:
        copy.wait()

    @pl.when(is_cap)
    def _():
        rows, lanes = tile_ids()
        b = lat_c[0]
        halo_row = pl.multiple_of(cap_row, 8)
        for k in range(3):
            for level in range(lev):
                at = 2 * (5 * level + k)
                body, tail = widen(
                    cap_raw[k, level], width,
                    got_e[pl.ds(halo_row, CAP + 8), :], got_w[pl.ds(halo_row, CAP + 8), :],
                    (e - at) % 128, (126 - at) % 128,
                )
                cap[k, level, 0:8, :] = jnp.zeros((8, width), jnp.float32)
                cap[k, level, 8 : CAP + 16, :last] = body
                cap[k, level, 8 : CAP + 16, last:] = tail
                cap[k, level, CAP + 16 : CAP + 24, :] = jnp.zeros((8, width), jnp.float32)
        first = jnp.where(band == 0, 8, 16)

        def level_body(level, _):
            def load(m, r, c):
                at = pl.multiple_of(r, 8)
                return cap[m, level, pl.ds(at, 8), 128 * c : 128 * c + 128]

            first_carry(load, first - 8, b, (0,), width // 128, carry)

            def body(i, _):
                pr = jnp.where(band == 0, 0, n_rows - CAP) + 8 * i
                a, f = eight_rows(courant, pr, rows), eight_rows(rotate, pr, rows)
                dst = pl.multiple_of(8 * i, 8)

                def emit(c, tends):
                    for k in range(3):
                        cap_t[k, level, pl.ds(dst, 8), 128 * c : 128 * c + 128] = tends[k]

                near = rolled(load, width // 128)
                chunk(load, near, first + 8 * i, a, f, b, (0,), width // 128, carry, emit)
                return 0

            lax.fori_loop(0, CAP // 8, body, 0, unroll=2)
            return 0

        lax.fori_loop(0, lev, level_body, 0)
        flat = cap_t[...].reshape(3 * lev * CAP, width)
        comp[...] = dot3(flat, uh[...], ul[...]).reshape(count, owned, RANK)

        def send(src, dst, sends, recvs, j):
            peer = lax.rem(me + j, count)
            return pltpu.make_async_remote_copy(
                src_ref=src.at[peer], dst_ref=dst.at[me],
                send_sem=sends.at[j], recv_sem=recvs.at[j], device_id={"lon": peer},
            )

        first_sends = [send(comp, mid_in, a_send, a_recv, j) for j in range(1, count)]
        for copy in first_sends:
            copy.start()
        mid_in[me] = comp[me]
        for copy in first_sends:
            copy.wait()
        gathered = jnp.concatenate([mid_in[s] for s in range(count)], 1)
        spectra = dot3(gathered, gh[...], gl[...])
        modes = lax.broadcasted_iota(jnp.int32, (owned, 2 * KEEP), 1)
        modes = jnp.where(modes >= KEEP, modes - KEEP, modes)
        full = cells * count
        weight = jnp.where(modes == 0, 1.0 / full, 2.0 / full).astype(jnp.float32)
        mode_rows = lax.broadcasted_iota(jnp.int32, (8, 2 * KEEP), 0)
        base = jnp.where(band == 0, 0, n_rows - CAP)
        limit = jnp.concatenate(
            [
                eight_rows(cuts, base + lax.rem(me * owned + 8 * g, CAP), mode_rows)
                for g in range(owned // 8)
            ],
            0,
        )
        spectra = jnp.where(modes <= limit, spectra * weight, 0.0)
        spread = dot3(spectra, th[...], tl[...])
        for s in range(count):
            mid_out[s] = spread[:, RANK * s : RANK * s + RANK]
        second_sends = [send(mid_out, coef, b_send, b_recv, j) for j in range(1, count)]
        for copy in second_sends:
            copy.start()
        coef[me] = mid_out[me]
        for copy in second_sends:
            copy.wait()
        out_coef[...] = coef[...].reshape(3 * lev * CAP, RANK)

    @pl.when(jnp.logical_not(is_cap))
    def _():
        out_coef[...] = jnp.zeros((3 * lev * CAP, RANK), jnp.float32)

    @pl.when(has_n)
    def _():
        to_north.wait_send()
        to_south_in = to_south
        to_south_in.wait_recv()
        out_north[...] = got_n[...]

    @pl.when(has_s)
    def _():
        to_south.wait_send()
        to_north.wait_recv()
        out_south[...] = got_s[...]

    @pl.when(jnp.logical_not(has_n))
    def _():
        out_north[...] = jnp.zeros(out_north.shape, jnp.float32)

    @pl.when(jnp.logical_not(has_s))
    def _():
        out_south[...] = jnp.zeros(out_south.shape, jnp.float32)


def step_kernel(geo, *refs):
    lev, n_rows, cells, width, count, bands = geo
    fields = refs[0:5]
    courant, rotate, mask, lat_c, east, west, north, south, coef, wh, wl, moves = refs[5:17]
    outs = refs[17:22]
    pad, ahead, beyond, carry = refs[22:26]
    level = pl.program_id(0)
    band = lax.axis_index("lat")
    last = width - 128
    e = cells - last
    rows, lanes = tile_ids()
    b = lat_c[0]
    tiles = width // 128
    zeros = jnp.zeros((8, 128), jnp.float32)
    for k in range(5):
        for c in range(tiles):
            stop = min(cells, 128 * c + 128)
            wide = stop - 128 * c
            pad[k, c, 0:8, :] = zeros
            pad[k, c, n_rows + 8 : n_rows + 16, :] = zeros
            pad[k, c, 6:8, :wide] = north[0, 2 * k : 2 * k + 2, 128 * c : stop]
            pad[k, c, n_rows + 8 : n_rows + 10, :wide] = south[0, 2 * k : 2 * k + 2, 128 * c : stop]
    for k in (3, 4):
        for r in (0, n_rows + 8):
            pad[k, :, r : r + 8, :] = pad[k, :, r : r + 8, :] * pad[0, :, r : r + 8, :]

    def fill(c, _):
        r = pl.multiple_of(8 * c, 8)
        to = pl.multiple_of(8 * c + 8, 8)
        ea, we = east[pl.ds(r, 8), :], west[pl.ds(r, 8), :]
        thick = None
        for k in range(5):
            at = 2 * (5 * level + k)
            body, tail = widen(
                fields[k][0, pl.ds(r, 8), :], width, ea, we,
                e + 128 - at, 126 - at,
            )
            if k == 0:
                thick = body, tail
            if k >= 3:
                body, tail = body * thick[0], tail * thick[1]
            for t in range(tiles - 1):
                pad[k, t, pl.ds(to, 8), :] = body[:, 128 * t : 128 * t + 128]
            pad[k, tiles - 1, pl.ds(to, 8), :] = tail
        return 0

    lax.fori_loop(0, n_rows // 8, fill, 0, unroll=4)

    def load(m, r, c):
        return pad[m, c, pl.ds(pl.multiple_of(r, 8), 8), :]

    depth = n_rows + 16
    for k in range(5):
        flat = pad[k].reshape(tiles * depth, 128)
        moved = jnp.dot(
            jnp.concatenate(halves(flat), 1),
            moves[1 if k in (1, 2) else 0],
            preferred_element_type=jnp.float32,
        )
        ahead[k] = moved[:, :128].reshape(tiles, depth, 128)
        beyond[k] = moved[:, 128:].reshape(tiles, depth, 128)

    by_roll = rolled(load, tiles)

    def near(m, r, c, k):
        wind = m in (1, 2)
        if k == -1 and not wind:
            return by_roll(m, r, c, k)
        at = pl.ds(pl.multiple_of(r, 8), 8)
        east, west = (c + 1) % tiles, (c + tiles - 1) % tiles
        if k == 1:
            return jnp.where(lanes < 127, ahead[m, c, at, :], ahead[m, east, at, :])
        if k == 2:
            return jnp.where(lanes < 126, beyond[m, c, at, :], beyond[m, east, at, :])
        return jnp.where(lanes > 0, beyond[m, c, at, :], beyond[m, west, at, :])

    masses = (0, 3, 4)
    first_carry(load, 0, b, masses, tiles, carry)

    def body(i, _):
        r = 8 * i + 8
        src = pl.multiple_of(8 * i, 8)
        a, f = eight_rows(courant, src, rows), eight_rows(rotate, src, rows)

        def emit(c, tends):
            stop = min(cells, 128 * c + 128)
            for k in range(5):
                new = load(k, r, c) + tends[k]
                outs[k][0, pl.ds(src, 8), 128 * c : stop] = new[:, : stop - 128 * c]

        chunk(load, near, r, a, f, b, masses, tiles, carry, emit)
        return 0

    lax.fori_loop(0, n_rows // 8, body, 0, unroll=2)

    @pl.when(jnp.logical_or(band == 0, band == bands - 1))
    def _():
        start = pl.multiple_of(jnp.where(band == 0, 0, n_rows - CAP), 8)
        flat = coef[...].reshape(3 * CAP, RANK)
        smooth = dot3(flat, wh[...], wl[...])
        wide_rows = lax.broadcasted_iota(jnp.int32, (8, cells), 0)
        flags = [eight_rows(mask, start + 8 * g, wide_rows) for g in range(CAP // 8)]
        chosen = jnp.concatenate(flags, 0) == 1
        for k in range(3):
            new = fields[k][0, pl.ds(start, CAP), :] + smooth[CAP * k : CAP * k + CAP, :cells]
            old = outs[k][0, pl.ds(start, CAP), :]
            outs[k][0, pl.ds(start, CAP), :] = jnp.where(chosen, new, old)


def local(thick, uwind, vwind, theta, moist, lon_courant, lat_courant, coriolis, cap_mask, cutoffs):
    lev, n_rows, cells = thick.shape
    count = lax.axis_size("lon")
    bands = lax.axis_size("lat")
    width = (cells + 4 + 127) // 128 * 128
    geo = (lev, n_rows, cells, width, count, bands)
    uh, ul, wh, wl, gh, gl, th, tl = (jnp.asarray(t) for t in tables(cells, count, width))
    fields = (thick, uwind, vwind, theta, moist)
    lat_c = lat_courant.reshape(1)
    moves = jnp.asarray(shift_tables())

    whole = lambda shape: pl.BlockSpec(shape, lambda i: (0,) * len(shape))
    smem = pl.BlockSpec(memory_space=pltpu.SMEM)
    edge = lambda col: pl.BlockSpec((lev, n_rows, 128), lambda i: (0, 0, col))
    owned = 3 * lev * CAP // count
    f32 = jnp.float32
    rows_all = 3 * lev * CAP
    dma = pltpu.SemaphoreType.DMA
    east, west, north, south, coef = pl.pallas_call(
        functools.partial(exchange_kernel, geo),
        grid=(1,),
        out_shape=(
            jax.ShapeDtypeStruct((n_rows, 128), f32),
            jax.ShapeDtypeStruct((n_rows, 128), f32),
            jax.ShapeDtypeStruct((lev, 10, cells), f32),
            jax.ShapeDtypeStruct((lev, 10, cells), f32),
            jax.ShapeDtypeStruct((rows_all, RANK), f32),
        ),
        in_specs=[edge(0)] * 5
        + [edge(cells // 128)] * 5
        + [pl.BlockSpec(memory_space=pl.ANY)] * 5
        + [smem] * 4
        + [whole(uh.shape)] * 2
        + [pl.BlockSpec(memory_space=pl.ANY)] * 4,
        out_specs=(
            whole((n_rows, 128)),
            whole((n_rows, 128)),
            whole((lev, 10, cells)),
            whole((lev, 10, cells)),
            whole((rows_all, RANK)),
        ),
        scratch_shapes=[pltpu.VMEM((n_rows, 128), f32)] * 4
        + [pltpu.VMEM((5, lev, 8, cells), f32)] * 2
        + [pltpu.VMEM((lev, 10, cells), f32)] * 4
        + [
            pltpu.VMEM((3, lev, CAP + 8, cells), f32),
            pltpu.VMEM((3, lev, CAP + 24, width), f32),
            pltpu.VMEM((3, lev, CAP, width), f32),
            pltpu.VMEM((1, 8, width), f32),
            pltpu.VMEM(gh.shape, jnp.bfloat16),
            pltpu.VMEM(gl.shape, jnp.bfloat16),
            pltpu.VMEM(th.shape, jnp.bfloat16),
            pltpu.VMEM(tl.shape, jnp.bfloat16),
        ]
        + [pltpu.VMEM((count, owned, RANK), f32)] * 4
        + [dma((17,))]
        + [dma((2,))] * 4
        + [dma((count,))] * 4,
        compiler_params=pltpu.CompilerParams(
            collective_id=0, has_side_effects=True, vmem_limit_bytes=VMEM_LIMIT
        ),
        name="exchange",
    )(*fields, *fields, *fields, lon_courant, coriolis, cutoffs, lat_c, uh, ul, gh, gl, th, tl)

    by_level = lambda shape: pl.BlockSpec(
        (1,) + shape, lambda i: (i,) + (0,) * len(shape)
    )
    coef = coef.reshape(3, lev, CAP, RANK)
    return pl.pallas_call(
        functools.partial(step_kernel, geo),
        grid=(lev,),
        out_shape=tuple(jax.ShapeDtypeStruct((lev, n_rows, cells), f32) for _ in range(5)),
        in_specs=[by_level((n_rows, cells))] * 5
        + [smem] * 4
        + [whole((n_rows, 128))] * 2
        + [by_level((10, cells))] * 2
        + [pl.BlockSpec((3, 1, CAP, RANK), lambda i: (0, i, 0, 0))]
        + [whole(wh.shape)] * 2
        + [whole(moves.shape)],
        out_specs=[by_level((n_rows, cells))] * 5,
        scratch_shapes=[
            *[pltpu.VMEM((5, width // 128, n_rows + 16, 128), f32)] * 3,
            pltpu.VMEM((3, 8, width), f32),
        ],
        compiler_params=pltpu.CompilerParams(vmem_limit_bytes=VMEM_LIMIT),
        name="substep",
    )(*fields, lon_courant, coriolis, cap_mask, lat_c, east, west, north, south, coef, wh, wl, moves)


def solution(mesh):
    field = P(None, "lat", "lon")
    row = P("lat")
    return jax.shard_map(
        local,
        mesh=mesh,
        in_specs=(field,) * 5 + (row, P(), row, row, row),
        out_specs=(field,) * 5,
        check_vma=False,
    )
```

```python
import functools
import math

import jax
import jax.numpy as jnp
import ml_dtypes
import numpy as np
from jax import lax
from jax.experimental import pallas as pl
from jax.experimental.pallas import tpu as pltpu
from jax.sharding import PartitionSpec as P

CAP = 32
KEEP = 256
RANK = 128
VMEM_LIMIT = 60 * 1024 * 1024


def split_table(table):
    table = np.asarray(table, np.float32)
    high = table.astype(ml_dtypes.bfloat16)
    low = (table - high.astype(np.float32)).astype(ml_dtypes.bfloat16)
    return high, low


@functools.lru_cache(maxsize=None)
def tables(cells, count, padded):
    full = cells * count
    t = np.arange(cells)
    band = (KEEP - 0.5) / full
    diag = ((cells - 1 - 2 * t) / 2.0) ** 2 * math.cos(2 * math.pi * band)
    off = t[1:] * (cells - t[1:]) / 2.0
    _, vectors = np.linalg.eigh(np.diag(diag) + np.diag(off, 1) + np.diag(off, -1))
    basis = vectors[:, ::-1][:, :RANK]
    basis = basis * np.where(basis[cells // 2 - 3] < 0, -1.0, 1.0)
    modes = np.arange(KEEP)
    blocks = []
    for s in range(count):
        phase = 2 * np.pi * (((s * cells + t)[:, None] * modes[None, :]) % full) / full
        blocks.append(basis.T @ np.concatenate([np.cos(phase), np.sin(phase)], 1))
    wide = np.zeros((padded, RANK))
    wide[:cells] = basis
    modal = np.concatenate(blocks, 0)
    return (
        split_table(wide) + split_table(wide.T) + split_table(modal) + split_table(modal.T)
    )


def halves(x):
    high = x.astype(jnp.bfloat16)
    return high, (x - high.astype(jnp.float32)).astype(jnp.bfloat16)


def dot3(x, high, low):
    dot = functools.partial(jnp.dot, preferred_element_type=jnp.float32)
    xh, xl = halves(x)
    rows = x.shape[0]
    both = dot(jnp.concatenate([xh, xl], 0), high)
    return both[:rows] + (both[rows:] + dot(xh, low))


def eight_rows(vector, first, rows):
    out = jnp.full(rows.shape, vector[first])
    for k in range(1, 8):
        out = jnp.where(rows == k, vector[first + k], out)
    return out


def row_up(cur, nxt, k, rows):
    return pltpu.roll(jnp.where(rows < k, nxt, cur), 8 - k, 0)


def row_down(cur, prv, k, rows):
    return pltpu.roll(jnp.where(rows >= 8 - k, prv, cur), k, 0)


def lane_up(cur, nxt, k, lanes):
    return pltpu.roll(jnp.where(lanes < k, nxt, cur), 128 - k, 1)


def lane_down(cur, prv, k, lanes):
    return pltpu.roll(jnp.where(lanes >= 128 - k, prv, cur), k, 1)


def tile_ids():
    return (
        lax.broadcasted_iota(jnp.int32, (8, 128), 0),
        lax.broadcasted_iota(jnp.int32, (8, 128), 1),
    )


def face_terms(speed):
    part = speed * (1.0 / 12.0)
    seven = 7.0 * part
    half = 0.5 * jnp.abs(speed)
    return seven + half, seven - half, part


def first_carry(load, r, b, masses, tiles, carry):
    rows, _ = tile_ids()
    for c in range(tiles):
        v, vn = load(2, r, c), load(2, r + 8, c)
        p, q, s = face_terms((0.5 * b) * (v + row_up(v, vn, 1, rows)))
        for k, m in enumerate(masses):
            cur, nxt = load(m, r, c), load(m, r + 8, c)
            carry[k, :, 128 * c : 128 * c + 128] = (
                p * cur
                + q * row_up(cur, nxt, 1, rows)
                - s * (row_down(cur, cur, 1, rows) + row_up(cur, nxt, 2, rows))
            )


def rolled(load, tiles):
    lanes = tile_ids()[1]

    def near(m, r, c, k):
        cur = load(m, r, c)
        if k > 0:
            return lane_up(cur, load(m, r, (c + 1) % tiles), k, lanes)
        return lane_down(cur, load(m, r, (c + tiles - 1) % tiles), -k, lanes)

    return near


def shift_tables():
    eye = np.eye(128)
    out = []
    for pair in ((1, 2), (1, -1)):
        moves = np.concatenate([np.roll(eye, -k, 0).T for k in pair], 1)
        out.append(np.concatenate([moves, moves], 0).astype(ml_dtypes.bfloat16))
    return np.stack(out)


def chunk(load, near, r, a, f, b, masses, tiles, carry, emit):
    rows, lanes = tile_ids()
    half_a = 0.5 * a

    def lon_part(c):
        ue = near(1, r, c, 1)
        p, q, s = face_terms(half_a * (load(1, r, c) + ue))
        fluxes, dh = [], None
        for m in masses:
            e, w = near(m, r, c, 1), near(m, r, c, -1)
            if m == 0:
                dh = e - w
            fluxes.append(p * load(m, r, c) + q * e - s * (w + near(m, r, c, 2)))
        return fluxes, dh, ue

    wrapped = lon_part(tiles - 1)
    before = wrapped[0]
    for c in range(tiles):
        fluxes, dh, ue = wrapped if c == tiles - 1 else lon_part(c)
        cols = slice(128 * c, 128 * c + 128)
        u, v = load(1, r, c), load(2, r, c)
        vn = row_up(v, load(2, r + 8, c), 1, rows)
        p, q, s = face_terms((0.5 * b) * (v + vn))
        tends = []
        dn = None
        for k, m in enumerate(masses):
            prv, cur, nxt = load(m, r - 8, c), load(m, r, c), load(m, r + 8, c)
            n, so = row_up(cur, nxt, 1, rows), row_down(cur, prv, 1, rows)
            if m == 0:
                dn = n - so
            up = p * cur + q * n - s * (so + row_up(cur, nxt, 2, rows))
            tends.append(
                lane_down(fluxes[k], before[k], 1, lanes)
                - fluxes[k]
                + (row_down(up, carry[k, :, cols], 1, rows) - up)
            )
            carry[k, :, cols] = up
        before = fluxes
        au, bv = half_a * u, (0.5 * b) * v
        du = row_up(u, load(1, r + 8, c), 1, rows) - row_down(u, load(1, r - 8, c), 1, rows)
        dv = vn - row_down(v, load(2, r - 8, c), 1, rows)
        tu = f * v - au * (ue - near(1, r, c, -1)) - bv * du - half_a * dh
        tv = -(f * u) - au * (near(2, r, c, 1) - near(2, r, c, -1)) - bv * dv - (0.5 * b) * dn
        emit(c, [tends[0], tu, tv] + tends[1:])


def widen(x, width, east, west, east_shift, west_shift):
    cells = x.shape[1]
    last = width - 128
    tail = jnp.concatenate(
        [x[:, last:], jnp.zeros((x.shape[0], width - cells), jnp.float32)], 1
    )
    ids = lax.broadcasted_iota(jnp.int32, (x.shape[0], 128), 1)
    e = cells - last
    moved = pltpu.roll(east, east_shift, 1)
    tail = jnp.where((ids >= e) & (ids < e + 2), moved, tail)
    if west is not None:
        moved = pltpu.roll(west, west_shift, 1)
    tail = jnp.where(ids >= 126, moved, tail)
    return x[:, :last], tail


def west_offset(e, lev):
    return 126 - e if 126 - e >= 10 * lev and 126 - e + 10 * lev <= 128 else 0


def exchange_kernel(geo, *refs):
    lev, n_rows, cells, width, count, bands = geo
    left, right = refs[0:5], refs[5:10]
    fields = refs[10:15]
    courant, rotate, cuts, lat_c, uh, ul = refs[15:21]
    in_hbm = refs[21:25]
    out_east, out_west, out_north, out_south, out_coef = refs[25:30]
    (
        send_w, send_e, got_e, got_w, edge_n, edge_s, send_n, send_s, got_n, got_s,
        cap_raw, cap, cap_t, carry, gh, gl, th, tl, comp, mid_in, mid_out, coef,
        in_sem, lon_send, lon_recv, lat_send, lat_recv, a_send, a_recv, b_send, b_recv,
    ) = refs[30:]
    me = lax.axis_index("lon")
    band = lax.axis_index("lat")
    has_n = band > 0
    has_s = band < bands - 1
    is_cap = jnp.logical_or(band == 0, band == bands - 1)
    last = width - 128
    e = cells - last
    owned = 3 * lev * CAP // count
    gap = west_offset(e, lev)

    barrier = pltpu.get_barrier_semaphore()
    for j in range(1, count):
        pl.semaphore_signal(barrier, inc=1, device_id={"lon": lax.rem(me + j, count)})

    @pl.when(has_n)
    def _():
        pl.semaphore_signal(barrier, inc=1, device_id={"lat": band - 1})

    @pl.when(has_s)
    def _():
        pl.semaphore_signal(barrier, inc=1, device_id={"lat": band + 1})

    cap_row = jnp.where(band == 0, 0, n_rows - CAP - 8)
    loads = []
    for k in range(5):
        loads.append(
            pltpu.make_async_copy(fields[k].at[:, pl.ds(0, 8), :], edge_n.at[k], in_sem.at[k])
        )
        loads.append(
            pltpu.make_async_copy(
                fields[k].at[:, pl.ds(n_rows - 8, 8), :], edge_s.at[k], in_sem.at[5 + k]
            )
        )
    cap_loads = [
        pltpu.make_async_copy(
            fields[k].at[:, pl.ds(pl.multiple_of(cap_row, 8), CAP + 8), :],
            cap_raw.at[k],
            in_sem.at[10 + k],
        )
        for k in range(3)
    ]
    table_loads = [
        pltpu.make_async_copy(src, dst, in_sem.at[13 + k])
        for k, (src, dst) in enumerate(zip(in_hbm, (gh, gl, th, tl)))
    ]
    for copy in loads + cap_loads + table_loads:
        copy.start()

    to_west = pltpu.make_async_remote_copy(
        src_ref=send_w, dst_ref=got_e, send_sem=lon_send.at[0], recv_sem=lon_recv.at[0],
        device_id={"lon": lax.rem(me + count - 1, count)},
    )
    to_east = pltpu.make_async_remote_copy(
        src_ref=send_e, dst_ref=got_w, send_sem=lon_send.at[1], recv_sem=lon_recv.at[1],
        device_id={"lon": lax.rem(me + 1, count)},
    )
    ids = lax.broadcasted_iota(jnp.int32, (n_rows, 128), 1)
    west_edge = jnp.zeros((n_rows, 128), jnp.float32)
    east_edge = jnp.zeros((n_rows, 128), jnp.float32)
    for level in range(lev):
        for k in range(5):
            at = 2 * (5 * level + k)
            here = (ids >= at) & (ids < at + 2)
            west_edge = jnp.where(here, pltpu.roll(left[k][level], at, 1), west_edge)
    send_w[...] = west_edge
    greeted = count - 1 + jnp.where(has_n, 1, 0) + jnp.where(has_s, 1, 0)
    pl.semaphore_wait(barrier, greeted)
    to_west.start()
    for level in range(lev):
        for k in range(5):
            at = 2 * (5 * level + k) + gap
            here = (ids >= at) & (ids < at + 2)
            east_edge = jnp.where(
                here, pltpu.roll(right[k][level], (at - (e - 2)) % 128, 1), east_edge
            )
    send_e[...] = east_edge
    to_east.start()

    for copy in loads:
        copy.wait()
    for k in range(5):
        for level in range(lev):
            send_n[level, 2 * k : 2 * k + 2, :] = edge_n[k, level, 0:2, :]
            send_s[level, 2 * k : 2 * k + 2, :] = edge_s[k, level, 6:8, :]
    to_north = pltpu.make_async_remote_copy(
        src_ref=send_n, dst_ref=got_s, send_sem=lat_send.at[0], recv_sem=lat_recv.at[0],
        device_id={"lat": lax.rem(band + bands - 1, bands)},
    )
    to_south = pltpu.make_async_remote_copy(
        src_ref=send_s, dst_ref=got_n, send_sem=lat_send.at[1], recv_sem=lat_recv.at[1],
        device_id={"lat": lax.rem(band + 1, bands)},
    )

    @pl.when(has_n)
    def _():
        to_north.start()

    @pl.when(has_s)
    def _():
        to_south.start()

    for copy in cap_loads:
        copy.wait()
    to_west.wait()
    to_east.wait()
    if gap:
        got_e[...] = got_e[...] + got_w[...]
    out_east[...] = got_e[...]
    out_west[...] = got_w[...]

    for copy in table_loads:
        copy.wait()

    @pl.when(is_cap)
    def _():
        rows, lanes = tile_ids()
        b = lat_c[0]
        halo_row = pl.multiple_of(cap_row, 8)
        for k in range(3):
            for level in range(lev):
                at = 2 * (5 * level + k)
                body, tail = widen(
                    cap_raw[k, level], width,
                    got_e[pl.ds(halo_row, CAP + 8), :],
                    None if gap else got_w[pl.ds(halo_row, CAP + 8), :],
                    (e - at) % 128, (126 - at) % 128,
                )
                cap[k, level, 0:8, :] = jnp.zeros((8, width), jnp.float32)
                cap[k, level, 8 : CAP + 16, :last] = body
                cap[k, level, 8 : CAP + 16, last:] = tail
                cap[k, level, CAP + 16 : CAP + 24, :] = jnp.zeros((8, width), jnp.float32)
        first = jnp.where(band == 0, 8, 16)

        def level_body(level, _):
            def load(m, r, c):
                at = pl.multiple_of(r, 8)
                return cap[m, level, pl.ds(at, 8), 128 * c : 128 * c + 128]

            first_carry(load, first - 8, b, (0,), width // 128, carry)

            def body(i, _):
                pr = jnp.where(band == 0, 0, n_rows - CAP) + 8 * i
                a, f = eight_rows(courant, pr, rows), eight_rows(rotate, pr, rows)
                dst = pl.multiple_of(8 * i, 8)

                def emit(c, tends):
                    for k in range(3):
                        cap_t[k, level, pl.ds(dst, 8), 128 * c : 128 * c + 128] = tends[k]

                near = rolled(load, width // 128)
                chunk(load, near, first + 8 * i, a, f, b, (0,), width // 128, carry, emit)
                return 0

            lax.fori_loop(0, CAP // 8, body, 0, unroll=2)
            return 0

        lax.fori_loop(0, lev, level_body, 0)
        flat = cap_t[...].reshape(3 * lev * CAP, width)
        comp[...] = dot3(flat, uh[...], ul[...]).reshape(count, owned, RANK)

        def send(src, dst, sends, recvs, j):
            peer = lax.rem(me + j, count)
            return pltpu.make_async_remote_copy(
                src_ref=src.at[peer], dst_ref=dst.at[me],
                send_sem=sends.at[j], recv_sem=recvs.at[j], device_id={"lon": peer},
            )

        first_sends = [send(comp, mid_in, a_send, a_recv, j) for j in range(1, count)]
        for copy in first_sends:
            copy.start()
        mid_in[me] = comp[me]
        for copy in first_sends:
            copy.wait()
        gathered = jnp.concatenate([mid_in[s] for s in range(count)], 1)
        spectra = dot3(gathered, gh[...], gl[...])
        modes = lax.broadcasted_iota(jnp.int32, (owned, 2 * KEEP), 1)
        modes = jnp.where(modes >= KEEP, modes - KEEP, modes)
        full = cells * count
        weight = jnp.where(modes == 0, 1.0 / full, 2.0 / full).astype(jnp.float32)
        mode_rows = lax.broadcasted_iota(jnp.int32, (8, 2 * KEEP), 0)
        base = jnp.where(band == 0, 0, n_rows - CAP)
        limit = jnp.concatenate(
            [
                eight_rows(cuts, base + lax.rem(me * owned + 8 * g, CAP), mode_rows)
                for g in range(owned // 8)
            ],
            0,
        )
        spectra = jnp.where(modes <= limit, spectra * weight, 0.0)
        spread = dot3(spectra, th[...], tl[...])
        for s in range(count):
            mid_out[s] = spread[:, RANK * s : RANK * s + RANK]
        second_sends = [send(mid_out, coef, b_send, b_recv, j) for j in range(1, count)]
        for copy in second_sends:
            copy.start()
        coef[me] = mid_out[me]
        for copy in second_sends:
            copy.wait()
        out_coef[...] = coef[...].reshape(3 * lev * CAP, RANK)

    @pl.when(jnp.logical_not(is_cap))
    def _():
        out_coef[...] = jnp.zeros((3 * lev * CAP, RANK), jnp.float32)

    @pl.when(has_n)
    def _():
        to_north.wait_send()
        to_south_in = to_south
        to_south_in.wait_recv()
        out_north[...] = got_n[...]

    @pl.when(has_s)
    def _():
        to_south.wait_send()
        to_north.wait_recv()
        out_south[...] = got_s[...]

    @pl.when(jnp.logical_not(has_n))
    def _():
        out_north[...] = jnp.zeros(out_north.shape, jnp.float32)

    @pl.when(jnp.logical_not(has_s))
    def _():
        out_south[...] = jnp.zeros(out_south.shape, jnp.float32)


def step_kernel(geo, *refs):
    lev, n_rows, cells, width, count, bands = geo
    fields = refs[0:5]
    courant, rotate, mask, lat_c, east, west, north, south, coef, wh, wl, moves = refs[5:17]
    outs = refs[17:22]
    pad, ahead, beyond, carry = refs[22:26]
    level = pl.program_id(0)
    band = lax.axis_index("lat")
    last = width - 128
    e = cells - last
    rows, lanes = tile_ids()
    b = lat_c[0]
    tiles = width // 128
    zeros = jnp.zeros((8, 128), jnp.float32)
    for k in range(5):
        for c in range(tiles):
            stop = min(cells, 128 * c + 128)
            wide = stop - 128 * c
            pad[k, c, 0:8, :] = zeros
            pad[k, c, n_rows + 8 : n_rows + 16, :] = zeros
            pad[k, c, 6:8, :wide] = north[0, 2 * k : 2 * k + 2, 128 * c : stop]
            pad[k, c, n_rows + 8 : n_rows + 10, :wide] = south[0, 2 * k : 2 * k + 2, 128 * c : stop]
    for k in (3, 4):
        for r in (0, n_rows + 8):
            pad[k, :, r : r + 8, :] = pad[k, :, r : r + 8, :] * pad[0, :, r : r + 8, :]

    def fill(c, _):
        r = pl.multiple_of(8 * c, 8)
        to = pl.multiple_of(8 * c + 8, 8)
        ea = east[pl.ds(r, 8), :]
        we = None if west_offset(e, lev) else west[pl.ds(r, 8), :]
        thick = None
        for k in range(5):
            at = 2 * (5 * level + k)
            body, tail = widen(
                fields[k][0, pl.ds(r, 8), :], width, ea, we,
                e + 128 - at, 126 - at,
            )
            if k == 0:
                thick = body, tail
            if k >= 3:
                body, tail = body * thick[0], tail * thick[1]
            for t in range(tiles - 1):
                pad[k, t, pl.ds(to, 8), :] = body[:, 128 * t : 128 * t + 128]
            pad[k, tiles - 1, pl.ds(to, 8), :] = tail
        return 0

    lax.fori_loop(0, n_rows // 8, fill, 0, unroll=4)

    def load(m, r, c):
        return pad[m, c, pl.ds(pl.multiple_of(r, 8), 8), :]

    depth = n_rows + 16
    for k in range(5):
        flat = pad[k].reshape(tiles * depth, 128)
        moved = jnp.dot(
            jnp.concatenate(halves(flat), 1),
            moves[1 if k in (1, 2) else 0],
            preferred_element_type=jnp.float32,
        )
        ahead[k] = moved[:, :128].reshape(tiles, depth, 128)
        beyond[k] = moved[:, 128:].reshape(tiles, depth, 128)

    by_roll = rolled(load, tiles)

    def near(m, r, c, k):
        wind = m in (1, 2)
        if k == -1 and not wind:
            return by_roll(m, r, c, k)
        at = pl.ds(pl.multiple_of(r, 8), 8)
        east, west = (c + 1) % tiles, (c + tiles - 1) % tiles
        if k == 1:
            return jnp.where(lanes < 127, ahead[m, c, at, :], ahead[m, east, at, :])
        if k == 2:
            return jnp.where(lanes < 126, beyond[m, c, at, :], beyond[m, east, at, :])
        return jnp.where(lanes > 0, beyond[m, c, at, :], beyond[m, west, at, :])

    masses = (0, 3, 4)
    first_carry(load, 0, b, masses, tiles, carry)

    def body(i, _):
        r = 8 * i + 8
        src = pl.multiple_of(8 * i, 8)
        a, f = eight_rows(courant, src, rows), eight_rows(rotate, src, rows)

        def emit(c, tends):
            stop = min(cells, 128 * c + 128)
            for k in range(5):
                new = load(k, r, c) + tends[k]
                outs[k][0, pl.ds(src, 8), 128 * c : stop] = new[:, : stop - 128 * c]

        chunk(load, near, r, a, f, b, masses, tiles, carry, emit)
        return 0

    lax.fori_loop(0, n_rows // 8, body, 0, unroll=2)

    @pl.when(jnp.logical_or(band == 0, band == bands - 1))
    def _():
        start = pl.multiple_of(jnp.where(band == 0, 0, n_rows - CAP), 8)
        flat = coef[...].reshape(3 * CAP, RANK)
        smooth = dot3(flat, wh[...], wl[...])
        wide_rows = lax.broadcasted_iota(jnp.int32, (8, cells), 0)
        flags = [eight_rows(mask, start + 8 * g, wide_rows) for g in range(CAP // 8)]
        chosen = jnp.concatenate(flags, 0) == 1
        for k in range(3):
            new = fields[k][0, pl.ds(start, CAP), :] + smooth[CAP * k : CAP * k + CAP, :cells]
            old = outs[k][0, pl.ds(start, CAP), :]
            outs[k][0, pl.ds(start, CAP), :] = jnp.where(chosen, new, old)


def local(thick, uwind, vwind, theta, moist, lon_courant, lat_courant, coriolis, cap_mask, cutoffs):
    lev, n_rows, cells = thick.shape
    count = lax.axis_size("lon")
    bands = lax.axis_size("lat")
    width = (cells + 4 + 127) // 128 * 128
    geo = (lev, n_rows, cells, width, count, bands)
    uh, ul, wh, wl, gh, gl, th, tl = (jnp.asarray(t) for t in tables(cells, count, width))
    fields = (thick, uwind, vwind, theta, moist)
    lat_c = lat_courant.reshape(1)
    moves = jnp.asarray(shift_tables())

    whole = lambda shape: pl.BlockSpec(shape, lambda i: (0,) * len(shape))
    smem = pl.BlockSpec(memory_space=pltpu.SMEM)
    edge = lambda col: pl.BlockSpec((lev, n_rows, 128), lambda i: (0, 0, col))
    owned = 3 * lev * CAP // count
    f32 = jnp.float32
    rows_all = 3 * lev * CAP
    dma = pltpu.SemaphoreType.DMA
    east, west, north, south, coef = pl.pallas_call(
        functools.partial(exchange_kernel, geo),
        grid=(1,),
        out_shape=(
            jax.ShapeDtypeStruct((n_rows, 128), f32),
            jax.ShapeDtypeStruct((n_rows, 128), f32),
            jax.ShapeDtypeStruct((lev, 10, cells), f32),
            jax.ShapeDtypeStruct((lev, 10, cells), f32),
            jax.ShapeDtypeStruct((rows_all, RANK), f32),
        ),
        in_specs=[edge(0)] * 5
        + [edge(cells // 128)] * 5
        + [pl.BlockSpec(memory_space=pl.ANY)] * 5
        + [smem] * 4
        + [whole(uh.shape)] * 2
        + [pl.BlockSpec(memory_space=pl.ANY)] * 4,
        out_specs=(
            whole((n_rows, 128)),
            whole((n_rows, 128)),
            whole((lev, 10, cells)),
            whole((lev, 10, cells)),
            whole((rows_all, RANK)),
        ),
        scratch_shapes=[pltpu.VMEM((n_rows, 128), f32)] * 4
        + [pltpu.VMEM((5, lev, 8, cells), f32)] * 2
        + [pltpu.VMEM((lev, 10, cells), f32)] * 4
        + [
            pltpu.VMEM((3, lev, CAP + 8, cells), f32),
            pltpu.VMEM((3, lev, CAP + 24, width), f32),
            pltpu.VMEM((3, lev, CAP, width), f32),
            pltpu.VMEM((1, 8, width), f32),
            pltpu.VMEM(gh.shape, jnp.bfloat16),
            pltpu.VMEM(gl.shape, jnp.bfloat16),
            pltpu.VMEM(th.shape, jnp.bfloat16),
            pltpu.VMEM(tl.shape, jnp.bfloat16),
        ]
        + [pltpu.VMEM((count, owned, RANK), f32)] * 4
        + [dma((17,))]
        + [dma((2,))] * 4
        + [dma((count,))] * 4,
        compiler_params=pltpu.CompilerParams(
            collective_id=0, has_side_effects=True, vmem_limit_bytes=VMEM_LIMIT
        ),
        name="exchange",
    )(*fields, *fields, *fields, lon_courant, coriolis, cutoffs, lat_c, uh, ul, gh, gl, th, tl)

    by_level = lambda shape: pl.BlockSpec(
        (1,) + shape, lambda i: (i,) + (0,) * len(shape)
    )
    coef = coef.reshape(3, lev, CAP, RANK)
    return pl.pallas_call(
        functools.partial(step_kernel, geo),
        grid=(lev,),
        out_shape=tuple(jax.ShapeDtypeStruct((lev, n_rows, cells), f32) for _ in range(5)),
        in_specs=[by_level((n_rows, cells))] * 5
        + [smem] * 4
        + [whole((n_rows, 128))] * 2
        + [by_level((10, cells))] * 2
        + [pl.BlockSpec((3, 1, CAP, RANK), lambda i: (0, i, 0, 0))]
        + [whole(wh.shape)] * 2
        + [whole(moves.shape)],
        out_specs=[by_level((n_rows, cells))] * 5,
        scratch_shapes=[
            *[pltpu.VMEM((5, width // 128, n_rows + 16, 128), f32)] * 3,
            pltpu.VMEM((3, 8, width), f32),
        ],
        compiler_params=pltpu.CompilerParams(vmem_limit_bytes=VMEM_LIMIT),
        name="substep",
    )(*fields, lon_courant, coriolis, cap_mask, lat_c, east, west, north, south, coef, wh, wl, moves)


def solution(mesh):
    field = P(None, "lat", "lon")
    row = P("lat")
    return jax.shard_map(
        local,
        mesh=mesh,
        in_specs=(field,) * 5 + (row, P(), row, row, row),
        out_specs=(field,) * 5,
        check_vma=False,
    )
```
